128 devices in a mesh: tm: 8 (over z, core), space: 16 (over x, y).
Axes of the slice: x: 4, y: 4, z: 4, core: 2. Of those that a mesh axis runs over, the one named last changes fastest.
Arguments:
- features: bfloat16 [8, 64, 1536, 512], P('tm', None, 'space'), may hold values from -6 to 6
- pre_act: bfloat16 [8, 64, 1536, 512], P('tm', None, 'space'), may hold values from -6 to 6
- cotangent: bfloat16 [8, 64, 1536, 512], P('tm', None, 'space'), may hold values from -6 to 6
- first_weight: bfloat16 [9, 64, 64], replicated, may hold values from -0.25 to 0.25
- second_weight: bfloat16 [9, 64, 64], replicated, may hold values from -0.25 to 0.25
- tile_mask: int32 [8, 48, 16], P('tm'), may hold values from 0 to 1, as said below
- tile_list: int32 [8, 512], P('tm', 'space'), may hold values from 0 to 47, as said below
Outputs:
- input_grad: bfloat16 [8, 64, 1536, 512], P('tm', None, 'space')
- first_grad: float32 [9, 64, 64], replicated
- second_grad: float32 [9, 64, 64], replicated
The draws below stay inside these ranges and needn't reach their ends.
Inputs may be any that keep to these rules, and one draw needn't show every extreme that they name: `tile_mask`: within each hour, every block of 3 tile rows holds at least 8 and at most 32 active tiles, and some block holds exactly 32; two blocks whose indices differ by half the number of blocks hold at most 40 active tiles together, and some such pair holds exactly that. In each hour one column has active tiles in the first and the last tile row of every block. `tile_list`: for each hour and block b, entries b * 32 to b * 32 + 31 are distinct local tile numbers of block b: first all its active tiles in increasing order, then inactive ones in increasing order.
All inputs are finite; a program needn't handle non-finite values.
Results may differ from the reference program's by a relative error of at most 0.0085.
Values may be sent and summed in bfloat16 or wider, within the bound.
A program may use at most 256 MiB of HBM per device.

```python
import math
import jax
import jax.numpy as jnp
from jax import lax

C = 64
TS = 32
TILE_ROWS_DEV = 3
TILE_COLS = 16
MOST = 32
LEAST = 8
HOURS = 8
TILE_ROWS = 48
ROWS = 1536
WIDTH = 512
CELLS = 6291456


def storm_tiles(key):
    blocks = TILE_ROWS // TILE_ROWS_DEV
    per_block = TILE_ROWS_DEV * TILE_COLS
    centre_key, column_key, score_key = jax.random.split(key, 3)
    centre = jax.random.randint(centre_key, (HOURS, 1), 0, blocks)
    column = jax.random.randint(column_key, (HOURS, 1, 1), 0, TILE_COLS)
    block_ids = jnp.arange(blocks, dtype=jnp.int32)[None, :]
    distance = jnp.abs(block_ids - centre)
    spread_reach = jnp.maximum(blocks - 2 * distance, 0)
    counts = LEAST + (MOST - LEAST) * spread_reach // blocks
    tile_ids = jnp.arange(per_block, dtype=jnp.int32)[None, None, :]
    tile_rows = tile_ids // TILE_COLS
    tile_cols = tile_ids % TILE_COLS
    forced = (tile_cols == column) & ((tile_rows == 0) | (tile_rows == TILE_ROWS_DEV - 1))
    raw_scores = jax.random.randint(score_key, (HOURS, blocks, per_block), 0, 1 << 20)
    priority = jnp.where(forced, tile_ids - per_block, raw_scores * per_block + tile_ids)
    ordering = jnp.argsort(priority, axis=2)
    ranking = jnp.argsort(ordering, axis=2)
    active = ranking < counts[:, :, None]
    listing = jnp.argsort(jnp.where(active, tile_ids, tile_ids + per_block), axis=2)[:, :, :MOST]
    mask_tiles = active.astype(jnp.int32).reshape(HOURS, blocks, TILE_ROWS_DEV, TILE_COLS).reshape(HOURS, TILE_ROWS, TILE_COLS)
    return (mask_tiles, listing.reshape(HOURS, blocks * MOST).astype(jnp.int32))


def draw_tile_mask(key, part):
    shared = storm_tiles(key)
    return shared[0]


def draw_tile_list(key, part):
    shared = storm_tiles(key)
    return shared[1]


def steps_of(own_key, dims, cuts, least, top_value):
    factor_of = 1.0
    for axis_at, parts in cuts:
        draws = jax.random.uniform(jax.random.fold_in(jax.random.fold_in(own_key, 6), axis_at), (parts,), jnp.float32, least / len(cuts), top_value / len(cuts))
        factor_of = factor_of * jnp.repeat(jnp.exp(draws), dims[axis_at] // parts).reshape((-1,) + (1,) * (len(dims) - 1 - axis_at))
    return factor_of


def centred(own_key, dims, width, bound, cuts=(), held_as=jnp.bfloat16):
    level = steps_of(own_key, dims, cuts, -0.22, 0.18) if cuts else 1.0
    drawn = jax.random.normal(own_key, dims, jnp.float32) * width * level
    return jnp.minimum(jnp.maximum(drawn, -bound), bound).astype(held_as)


def setup_inputs(seed: int = 0) -> dict:
    arg_keys = jax.random.split(jax.random.key(seed), 8)
    features = centred(arg_keys[0], (HOURS, C, ROWS, WIDTH), 1.0, 6.0, ((0, 8), (2, 16)))
    pre_act = centred(arg_keys[1], (HOURS, C, ROWS, WIDTH), 1.0, 6.0, ((0, 8), (2, 16)))
    cotangent = centred(arg_keys[2], (HOURS, C, ROWS, WIDTH), 1.0, 6.0, ((0, 8), (2, 16)))
    first_weight = centred(arg_keys[3], (9, C, C), (9 * C) ** -0.5, 0.25)
    second_weight = centred(arg_keys[4], (9, C, C), (9 * C) ** -0.5, 0.25)
    tile_mask = draw_tile_mask(jax.random.fold_in(arg_keys[7], 71), 0)
    tile_list = draw_tile_list(jax.random.fold_in(arg_keys[7], 71), 0)
    return dict(features=features, pre_act=pre_act, cotangent=cotangent, first_weight=first_weight, second_weight=second_weight, tile_mask=tile_mask, tile_list=tile_list)


def highest_dot(left, right):
    return jnp.dot(left, right, precision=lax.Precision.HIGHEST, preferred_element_type=jnp.float32)

def window_stack(framed_field, tile_row, tile_col):
    anchor = jnp.zeros((), jnp.int32)
    window = lax.dynamic_slice(framed_field, (anchor, tile_row * TS, tile_col * TS), (C, TS + 2, TS + 2))
    pieces = []
    for step_row in (-1, 0, 1):
        for step_col in (-1, 0, 1):
            shifted = window[:, 1 - step_row:1 - step_row + TS, 1 - step_col:1 - step_col + TS]
            pieces.append(shifted.reshape(C, TS * TS).astype(jnp.float32))
    return jnp.concatenate(pieces, axis=0)

def tile_of(dense_field, tile_row, tile_col):
    anchor = jnp.zeros((), jnp.int32)
    return lax.dynamic_slice(dense_field, (anchor, tile_row * TS, tile_col * TS), (C, TS, TS)).reshape(C, TS * TS)

def put_tile(dense_field, tile_values, tile_row, tile_col):
    anchor = jnp.zeros((), jnp.int32)
    return lax.dynamic_update_slice(dense_field, tile_values.reshape(C, TS, TS), (anchor, tile_row * TS, tile_col * TS))

def reference(features, pre_act, cotangent, first_weight, second_weight, tile_mask, tile_list):
    blocks = TILE_ROWS // TILE_ROWS_DEV
    per_block = TILE_ROWS_DEV * TILE_COLS
    listing = tile_list.reshape(HOURS, blocks, MOST)
    matches = listing[:, :, :, None] == jnp.arange(per_block, dtype=jnp.int32)[None, None, None, :]
    listed = jnp.any(matches, axis=2).astype(jnp.int32)
    listed = listed.reshape(HOURS, blocks, TILE_ROWS_DEV, TILE_COLS).reshape(HOURS, TILE_ROWS, TILE_COLS)
    live_tiles = tile_mask * listed
    second_rows = second_weight.astype(jnp.float32).transpose(2, 0, 1).reshape(C, 9 * C)
    first_rows = first_weight.astype(jnp.float32).transpose(2, 0, 1).reshape(C, 9 * C)
    slot_block = jnp.arange(blocks * MOST, dtype=jnp.int32) // MOST

    def hour_backward(operands):
        input_hour, pre_hour, grad_hour, live_hour, list_hour = operands
        cell_mask = jnp.repeat(jnp.repeat(live_hour, TS, axis=0), TS, axis=1)[None].astype(jnp.bfloat16)
        grad_out = grad_hour * cell_mask
        kept_field = jnp.maximum(pre_hour, jnp.zeros((), pre_hour.dtype)) * cell_mask
        input_kept = input_hour * cell_mask
        tile_rows = slot_block * TILE_ROWS_DEV + list_hour // TILE_COLS
        tile_cols = list_hour % TILE_COLS
        live_slots = live_hour[tile_rows, tile_cols]
        grad_frame = jnp.pad(grad_out, ((0, 0), (1, 1), (1, 1)))
        zero_grad = jnp.zeros((9 * C, C), jnp.float32)

        def second_step(loop_carry, slot_info):
            tile_row, tile_col, live_flag = slot_info

            def active(loop_state):
                grad_sum, pre_grad = loop_state
                stacked = window_stack(grad_frame, tile_row, tile_col)
                kept_tile = tile_of(kept_field, tile_row, tile_col).astype(jnp.float32)
                upstream = highest_dot(second_rows, stacked)
                pre_tile = (upstream * (kept_tile > 0)).astype(jnp.bfloat16)
                grad_sum = grad_sum + highest_dot(stacked, kept_tile.T)
                return (grad_sum, put_tile(pre_grad, pre_tile, tile_row, tile_col))
            return (lax.cond(live_flag > 0, active, lambda loop_state: loop_state, loop_carry), None)
        (second_sum, pre_grad), unused_out = lax.scan(second_step, (zero_grad, jnp.zeros_like(grad_out)), (tile_rows, tile_cols, live_slots))
        pre_frame = jnp.pad(pre_grad, ((0, 0), (1, 1), (1, 1)))

        def first_step(loop_carry, slot_info):
            tile_row, tile_col, live_flag = slot_info

            def active(loop_state):
                grad_sum, input_grad = loop_state
                stacked = window_stack(pre_frame, tile_row, tile_col)
                input_tile = tile_of(input_kept, tile_row, tile_col).astype(jnp.float32)
                result_tile = highest_dot(first_rows, stacked).astype(jnp.bfloat16)
                grad_sum = grad_sum + highest_dot(stacked, input_tile.T)
                return (grad_sum, put_tile(input_grad, result_tile, tile_row, tile_col))
            return (lax.cond(live_flag > 0, active, lambda loop_state: loop_state, loop_carry), None)
        (first_sum, input_grad), unused_out = lax.scan(first_step, (zero_grad, jnp.zeros_like(input_hour)), (tile_rows, tile_cols, live_slots))
        return (input_grad, first_sum, second_sum)
    input_grad, first_parts, second_parts = lax.map(hour_backward, (features, pre_act, cotangent, live_tiles, tile_list))
    grad_scale = 1.0 / math.sqrt(CELLS)
    first_grad = (lax.optimization_barrier(jnp.sum(first_parts, axis=0)) * grad_scale).reshape(9, C, C)
    second_grad = (lax.optimization_barrier(jnp.sum(second_parts, axis=0)) * grad_scale).reshape(9, C, C)
    return (input_grad, first_grad, second_grad)
```

```python
import math

import jax
import jax.numpy as jnp
from jax import lax
from jax.experimental import pallas as pl
from jax.experimental.pallas import tpu as pltpu
from jax.sharding import PartitionSpec as P

F32 = jnp.float32
BF = jnp.bfloat16
C = 64
TS = 32
ROWS = 96
WIDTH = 512
STRIP = 16
STRIPS = ROWS // STRIP
PAIR = 2 * C
PAIRS = ROWS // 2
TM = 8
SPACE = 16
CHUNK = 3 * C // TM
NT = (((1,), (1,)), ((), ()))
MESH = pl.DeviceIdType.MESH
ORDER = (1, 0, -1)


def al(x, m=C):
    return x if isinstance(x, int) else pl.multiple_of(x, m)


def shift_right(x):
    lane = lax.broadcasted_iota(jnp.int32, (x.shape[0], 128), 1)
    out, carry = [], None
    for j in range(x.shape[1] // 128):
        r = pltpu.roll(x[:, j * 128 : (j + 1) * 128], 1, 1)
        out.append(jnp.where(lane == 0, jnp.zeros_like(r) if carry is None else carry, r))
        carry = r
    return jnp.concatenate(out, axis=1)


def shift_left(x):
    lane = lax.broadcasted_iota(jnp.int32, (x.shape[0], 128), 1)
    out, carry = [], None
    for j in reversed(range(x.shape[1] // 128)):
        r = pltpu.roll(x[:, j * 128 : (j + 1) * 128], 127, 1)
        out.append(jnp.where(lane == 127, jnp.zeros_like(r) if carry is None else carry, r))
        carry = r
    return jnp.concatenate(out[::-1], axis=1)


def build_weight(w_ref, out_ref):
    zero = jnp.zeros((C, C), F32)
    rows = []
    for q in range(4):
        cols = []
        for dc in ORDER:
            for t in range(2):
                dr = t + 1 - q
                cols.append(w_ref[(dr + 1) * 3 + dc + 1].astype(F32) if abs(dr) <= 1 else zero)
        rows.append(jnp.concatenate(cols, axis=1))
    out_ref[...] = jnp.concatenate(rows, axis=0).T.astype(BF)


def build_mask(mask_ref, out_ref):
    first = lax.axis_index("space") * (ROWS // TS)
    count, cols = mask_ref.shape
    pick = lax.broadcasted_iota(jnp.int32, (8, count), 0) + first
    pick = (pick == lax.broadcasted_iota(jnp.int32, (8, count), 1)).astype(F32).astype(BF)
    own = jnp.dot(pick, mask_ref[...].astype(F32).astype(BF), preferred_element_type=F32)
    spread = lax.broadcasted_iota(jnp.int32, (cols, WIDTH), 1) >> 5
    spread = (spread == lax.broadcasted_iota(jnp.int32, (cols, WIDTH), 0)).astype(F32).astype(BF)
    out_ref[...] = jnp.dot(own.astype(BF), spread, preferred_element_type=F32)


def conv_pair(weight, src_ref, base):
    part = jnp.dot(weight, src_ref[pl.ds(al(base), 2 * PAIR), :], preferred_element_type=F32)
    return shift_right(part[:PAIR]) + part[PAIR : 2 * PAIR] + shift_left(part[2 * PAIR :])


def grad_pair(own_ref, own_base, src_ref, base):
    own = own_ref[pl.ds(al(own_base), PAIR), :]
    own = jnp.concatenate([shift_right(own), own, shift_left(own)], axis=0)
    return lax.dot_general(own, src_ref[pl.ds(al(base), 2 * PAIR), :], NT, preferred_element_type=F32)


def main_kernel(
    cot_hbm, pre_hbm, feat_hbm, w2_ref, mask_ref, p_hbm, total_ref,
    cot_in, pre_in, feat_in, g, kept, inp, pgrad, weight, cells, acc2, acc1,
    part, gathered, scattered, summed,
    in_sem, out_sem, halo_send, halo_recv, rs_send, rs_recv, sp_send, sp_recv, ag_send, ag_recv,
):
    tm = lax.axis_index("tm")
    sp = lax.axis_index("space")
    up, down = lax.rem(sp + SPACE - 1, SPACE), lax.rem(sp + 1, SPACE)
    sources = ((cot_hbm, cot_in), (pre_hbm, pre_in), (feat_hbm, feat_in))

    def fetch(a, s):
        src, dst = sources[a]
        rows = pl.ds(al(s * STRIP, STRIP), STRIP)
        return pltpu.make_async_copy(src.at[:, rows, :], dst.at[:, rows, :], in_sem.at[a, s])

    for s in (0, STRIPS - 1):
        fetch(0, s).start()
        fetch(1, s).start()
    for s in range(1, STRIPS - 1):
        fetch(0, s).start()
        fetch(1, s).start()
    for s in range(STRIPS):
        fetch(2, s).start()

    barrier = pltpu.get_barrier_semaphore()
    for j in range(1, TM):
        pl.semaphore_signal(barrier, inc=1, device_id=(lax.rem(tm + j, TM), sp), device_id_type=MESH)
    for j in range(1, SPACE):
        pl.semaphore_signal(barrier, inc=1, device_id=(tm, lax.rem(sp + j, SPACE)), device_id_type=MESH)

    build_mask(mask_ref, cells)
    build_weight(w2_ref, weight)
    acc2[...] = jnp.zeros_like(acc2)
    acc1[...] = jnp.zeros_like(acc1)

    def strip_of(ref, s):
        mask = cells[pl.ds(s // 2, 1), :].astype(BF)
        return ref[:, pl.ds(al(s * STRIP, STRIP), STRIP), :], mask[None]

    def put(ref, first_row, s, x):
        x = jnp.transpose(x, (1, 0, 2)).reshape(STRIP * C, WIDTH)
        ref[pl.ds(al((s * STRIP + first_row) * C), STRIP * C), :] = x

    def load_cot_pre(s):
        x, mask = strip_of(cot_in, s)
        put(g, 2, s, x * mask)
        x, mask = strip_of(pre_in, s)
        put(kept, 1, s, jnp.maximum(x, jnp.zeros((), BF)) * mask)

    def load_feat(s):
        x, mask = strip_of(feat_in, s)
        put(inp, 0, s, x * mask)

    for s in (0, STRIPS - 1):
        fetch(0, s).wait()
        fetch(1, s).wait()
        load_cot_pre(s)

    pl.semaphore_wait(barrier, TM + SPACE - 2)

    def halo(i, ref, src_row, dst_row, count, to):
        return pltpu.make_async_remote_copy(
            src_ref=ref.at[pl.ds(src_row * C, count * C), :],
            dst_ref=ref.at[pl.ds(dst_row * C, count * C), :],
            send_sem=halo_send.at[i],
            recv_sem=halo_recv.at[i],
            device_id=(tm, to),
            device_id_type=MESH,
        )

    halos = (
        halo(0, g, 2, ROWS + 2, 2, up),
        halo(1, g, ROWS, 0, 2, down),
        halo(2, kept, 1, ROWS + 1, 1, up),
        halo(3, kept, ROWS, 0, 1, down),
    )
    for h in halos:
        h.start()

    fetch(0, 1).wait()
    fetch(1, 1).wait()
    load_cot_pre(1)

    def second_conv(p):
        base = p * PAIR
        out = conv_pair(weight[...], g, base).astype(BF)
        positive = kept[pl.ds(al(base), PAIR), :] > 0
        pgrad[pl.ds(al(base), PAIR), :] = jnp.where(positive, out, jnp.zeros((), BF))

    def second_grad(p):
        base = p * PAIR + C
        acc2[...] += grad_pair(kept, base, g, base)

    def pass1(s):
        for q in range(1, STRIP // 2 + 1):
            second_conv(s * (STRIP // 2) + q)
            second_grad(s * (STRIP // 2) + q)

    def body1(s, carry):
        fetch(0, s + 2).wait()
        fetch(1, s + 2).wait()
        load_cot_pre(s + 2)
        pass1(s)
        return carry

    lax.fori_loop(0, STRIPS - 3, body1, 0)

    def body1_late(s, carry):
        pass1(s)
        return carry

    lax.fori_loop(STRIPS - 3, STRIPS - 1, body1_late, 0)

    for h in halos:
        h.wait()

    @pl.when(sp == 0)
    def _():
        g[pl.ds(0, 2 * C), :] = jnp.zeros((2 * C, WIDTH), BF)
        kept[pl.ds(0, C), :] = jnp.zeros((C, WIDTH), BF)

    @pl.when(sp == SPACE - 1)
    def _():
        g[pl.ds((ROWS + 2) * C, 2 * C), :] = jnp.zeros((2 * C, WIDTH), BF)
        kept[pl.ds((ROWS + 1) * C, C), :] = jnp.zeros((C, WIDTH), BF)

    for q in range(PAIRS - 7, PAIRS):
        second_conv(q)
        second_grad(q)
    for q in (0, PAIRS):
        second_conv(q)
    second_grad(0)

    save = pltpu.make_async_copy(pgrad, p_hbm, out_sem)
    save.start()

    fetch(2, 0).wait()
    load_feat(0)

    def pass2(s):
        for q in range(STRIP // 2):
            base = (s * (STRIP // 2) + q) * PAIR
            acc1[...] += grad_pair(inp, base, pgrad, base)

    def body2(s, carry):
        fetch(2, s + 1).wait()
        load_feat(s + 1)
        pass2(s)
        return carry

    lax.fori_loop(0, STRIPS - 1, body2, 0)
    pass2(STRIPS - 1)

    for s in range(3):
        both = []
        for acc in (acc1, acc2):
            top = acc[pl.ds(s * PAIR, C), :][:, : 3 * C]
            both.append(top + acc[pl.ds(s * PAIR + C, C), :][:, C:])
        both = jnp.concatenate(both, axis=1)
        for r in range(0, C, 8):
            row = s * C + r
            part[row // CHUNK, pl.ds(row % CHUNK, 8), :] = both[r : r + 8]

    def exchange(src, dst, send, recv, slot, to):
        return pltpu.make_async_remote_copy(
            src_ref=src, dst_ref=dst, send_sem=send.at[slot], recv_sem=recv.at[slot],
            device_id=to, device_id_type=MESH,
        )

    copies = []
    for j in range(1, TM):
        t = lax.rem(tm + j, TM)
        copies.append(exchange(part.at[t], scattered.at[j - 1], rs_send, rs_recv, j - 1, (t, sp)))
        copies[-1].start()
    for c in copies:
        c.wait()
    mine = part[tm]
    for j in range(TM - 1):
        mine = mine + scattered[j]
    summed[...] = mine

    peers = [lax.rem(sp + j, SPACE) for j in range(1, SPACE)]
    sends = [
        pltpu.make_async_remote_copy(
            src_ref=summed, dst_ref=gathered.at[sp], send_sem=sp_send.at[j], recv_sem=sp_recv.at[sp],
            device_id=(tm, to), device_id_type=MESH,
        )
        for j, to in enumerate(peers)
    ]
    for c in sends:
        c.start()
    gathered[sp] = mine
    for c in sends:
        c.wait_send()
    for peer in peers:
        pltpu.make_async_remote_copy(
            src_ref=summed, dst_ref=gathered.at[peer], send_sem=sp_send.at[0], recv_sem=sp_recv.at[peer],
            device_id=(tm, peer), device_id_type=MESH,
        ).wait_recv()
    whole = gathered[0]
    for j in range(1, SPACE):
        whole = whole + gathered[j]
    total_ref[tm] = whole

    peers = [lax.rem(tm + j, TM) for j in range(1, TM)]
    sends = [
        pltpu.make_async_remote_copy(
            src_ref=total_ref.at[tm], dst_ref=total_ref.at[tm], send_sem=ag_send.at[j], recv_sem=ag_recv.at[tm],
            device_id=(to, sp), device_id_type=MESH,
        )
        for j, to in enumerate(peers)
    ]
    for c in sends:
        c.start()
    for c in sends:
        c.wait_send()
    for peer in peers:
        pltpu.make_async_remote_copy(
            src_ref=total_ref.at[tm], dst_ref=total_ref.at[peer], send_sem=ag_send.at[0], recv_sem=ag_recv.at[peer],
            device_id=(peer, sp), device_id_type=MESH,
        ).wait_recv()
    save.wait()


def last_kernel(
    p_hbm, w1_ref, mask_ref, total_ref, out_hbm, first_ref, second_ref,
    pgrad, rows, outs, weight, cells, in_sem, out_sem,
):
    def fetch(s):
        start, size = (0, (STRIP + 2) * C) if s == 0 else ((s * STRIP + 2) * C, STRIP * C)
        return pltpu.make_async_copy(p_hbm.at[pl.ds(start, size), :], pgrad.at[pl.ds(start, size), :], in_sem.at[s])

    for s in range(STRIPS):
        fetch(s).start()
    build_mask(mask_ref, cells)
    build_weight(w1_ref, weight)

    def store(s):
        r = pl.ds(al(s * STRIP, STRIP), STRIP)
        return pltpu.make_async_copy(outs.at[:, r, :], out_hbm.at[:, r, :], out_sem.at[s])

    for s in range(STRIPS):
        fetch(s).wait()
        mask = cells[pl.ds(s // 2, 1), :]
        for q in range(STRIP // 2):
            base = (s * (STRIP // 2) + q) * PAIR
            rows[pl.ds(base, PAIR), :] = (conv_pair(weight[...], pgrad, base) * mask).astype(BF)
        x = rows[pl.ds(s * STRIP * C, STRIP * C), :].reshape(STRIP, C, WIDTH)
        outs[:, pl.ds(s * STRIP, STRIP), :] = jnp.transpose(x, (1, 0, 2))
        store(s).start()

    scale = 1.0 / math.sqrt(TM * ROWS * SPACE * WIDTH)
    grid = total_ref[...].T * scale
    for n, ref in enumerate((first_ref, second_ref)):
        for q in range(3):
            row = (n * 3 + q) * C
            for s in range(3):
                ref[(2 - q) * 3 + s] = grid[row : row + C, s * C : (s + 1) * C]
    for s in range(STRIPS):
        store(s).wait()


def block(features, pre_act, cotangent, first_weight, second_weight, tile_mask, tile_list):
    vmem = pl.BlockSpec(memory_space=pltpu.VMEM)
    hbm = pl.BlockSpec(memory_space=pl.ANY)
    shape = (C, ROWS, WIDTH)
    mask = tile_mask[0]
    chunk = (CHUNK, 6 * C)
    dma = pltpu.SemaphoreType.DMA
    pgrad, total = pl.pallas_call(
        main_kernel,
        out_shape=(
            jax.ShapeDtypeStruct(((ROWS + 2) * C, WIDTH), BF),
            jax.ShapeDtypeStruct((TM,) + chunk, F32),
        ),
        in_specs=[hbm, hbm, hbm, vmem, vmem],
        out_specs=(hbm, vmem),
        scratch_shapes=[
            pltpu.VMEM(shape, BF),
            pltpu.VMEM(shape, BF),
            pltpu.VMEM(shape, BF),
            pltpu.VMEM(((ROWS + 4) * C, WIDTH), BF),
            pltpu.VMEM(((ROWS + 2) * C, WIDTH), BF),
            pltpu.VMEM((ROWS * C, WIDTH), BF),
            pltpu.VMEM(((ROWS + 2) * C, WIDTH), BF),
            pltpu.VMEM((3 * PAIR, 2 * PAIR), BF),
            pltpu.VMEM((8, WIDTH), F32),
            pltpu.VMEM((3 * PAIR, 2 * PAIR), F32),
            pltpu.VMEM((3 * PAIR, 2 * PAIR), F32),
            pltpu.VMEM((TM,) + chunk, F32),
            pltpu.VMEM((SPACE,) + chunk, F32),
            pltpu.VMEM((TM - 1,) + chunk, F32),
            pltpu.VMEM(chunk, F32),
            dma((3, STRIPS)),
            dma(()),
            dma((4,)),
            dma((4,)),
            dma((TM - 1,)),
            dma((TM - 1,)),
            dma((SPACE,)),
            dma((SPACE,)),
            dma((TM,)),
            dma((TM,)),
        ],
        compiler_params=pltpu.CompilerParams(
            collective_id=0, has_side_effects=True, vmem_limit_bytes=60 * 2**20
        ),
        name="grads",
    )(cotangent[0], pre_act[0], features[0], second_weight, mask)
    grad, first, second = pl.pallas_call(
        last_kernel,
        out_shape=(
            jax.ShapeDtypeStruct(shape, BF),
            jax.ShapeDtypeStruct((9, C, C), F32),
            jax.ShapeDtypeStruct((9, C, C), F32),
        ),
        in_specs=[hbm, vmem, vmem, vmem],
        out_specs=(hbm, vmem, vmem),
        scratch_shapes=[
            pltpu.VMEM(((ROWS + 2) * C, WIDTH), BF),
            pltpu.VMEM((ROWS * C, WIDTH), BF),
            pltpu.VMEM(shape, BF),
            pltpu.VMEM((3 * PAIR, 2 * PAIR), BF),
            pltpu.VMEM((8, WIDTH), F32),
            dma((STRIPS,)),
            dma((STRIPS,)),
        ],
        compiler_params=pltpu.CompilerParams(vmem_limit_bytes=60 * 2**20),
        name="input_grad",
    )(pgrad, first_weight, mask, total.reshape(TM * CHUNK, 6 * C))
    return grad[None], first, second


def solution(mesh):
    return jax.shard_map(
        block,
        mesh=mesh,
        in_specs=(
            P("tm", None, "space", None),
            P("tm", None, "space", None),
            P("tm", None, "space", None),
            P(),
            P(),
            P("tm", None, None),
            P("tm", "space"),
        ),
        out_specs=(P("tm", None, "space", None), P(), P()),
        check_vma=False,
    )
```

```python
import math

import jax
import jax.numpy as jnp
from jax import lax
from jax.experimental import pallas as pl
from jax.experimental.pallas import tpu as pltpu
from jax.sharding import PartitionSpec as P

F32 = jnp.float32
BF = jnp.bfloat16
C = 64
TS = 32
ROWS = 96
WIDTH = 512
STRIP = 16
STRIPS = ROWS // STRIP
PAIR = 2 * C
PAIRS = ROWS // 2
TM = 8
SPACE = 16
HALF = STRIP // 2
LANES = 128
GRAD_ROWS = 9 * C // 2
USED = 2 * GRAD_ROWS // TM
CHUNK = 80
RING = 4
PARTS = 8
NT = (((1,), (1,)), ((), ()))
MESH = pl.DeviceIdType.MESH
ORDER = (1, 0, -1)


def al(x, m=C):
    return x if isinstance(x, int) else pl.multiple_of(x, m)


def shift_right(x):
    lane = lax.broadcasted_iota(jnp.int32, (x.shape[0], 128), 1)
    out, carry = [], None
    for j in range(x.shape[1] // 128):
        r = pltpu.roll(x[:, j * 128 : (j + 1) * 128], 1, 1)
        out.append(jnp.where(lane == 0, jnp.zeros_like(r) if carry is None else carry, r))
        carry = r
    return jnp.concatenate(out, axis=1)


def shift_left(x):
    lane = lax.broadcasted_iota(jnp.int32, (x.shape[0], 128), 1)
    out, carry = [], None
    for j in reversed(range(x.shape[1] // 128)):
        r = pltpu.roll(x[:, j * 128 : (j + 1) * 128], 127, 1)
        out.append(jnp.where(lane == 127, jnp.zeros_like(r) if carry is None else carry, r))
        carry = r
    return jnp.concatenate(out[::-1], axis=1)


def build_weight(w_ref, out_ref):
    zero = jnp.zeros((C, C), F32)
    rows = []
    for q in range(4):
        cols = []
        for dc in ORDER:
            for t in range(2):
                dr = t + 1 - q
                cols.append(w_ref[(dr + 1) * 3 + dc + 1].astype(F32) if abs(dr) <= 1 else zero)
        rows.append(jnp.concatenate(cols, axis=1))
    out_ref[...] = jnp.concatenate(rows, axis=0).T.astype(BF)


def build_mask(mask_ref, out_ref):
    first = lax.axis_index("space") * (ROWS // TS)
    cols, count = mask_ref.shape
    pick = lax.broadcasted_iota(jnp.int32, (8, count), 0) + first
    pick = (pick == lax.broadcasted_iota(jnp.int32, (8, count), 1)).astype(F32).astype(BF)
    own = lax.dot_general(pick, mask_ref[...].astype(F32).astype(BF), NT, preferred_element_type=F32)
    spread = lax.broadcasted_iota(jnp.int32, (cols, WIDTH), 1) >> 5
    spread = (spread == lax.broadcasted_iota(jnp.int32, (cols, WIDTH), 0)).astype(F32).astype(BF)
    out_ref[...] = jnp.dot(own.astype(BF), spread, preferred_element_type=F32)


def conv_pair(weight, src_ref, base):
    part = jnp.dot(weight, src_ref[pl.ds(al(base), 2 * PAIR), :], preferred_element_type=F32)
    return shift_right(part[:PAIR]) + part[PAIR : 2 * PAIR] + shift_left(part[2 * PAIR :])


def grad_pair(own_ref, own_base, src_ref, base):
    own = own_ref[pl.ds(al(own_base), PAIR), :]
    own = jnp.concatenate([shift_right(own), own, shift_left(own)], axis=0)
    return lax.dot_general(own, src_ref[pl.ds(al(base), 2 * PAIR), :], NT, preferred_element_type=F32)


def main_kernel(
    cot_hbm, pre_hbm, feat_hbm, w2_ref, w1_ref, mask_ref, out_hbm, total_ref,
    cot_in, pre_in, feat_in, g, kept, inp, pgrad, weight2, weight1, cells, acc2, acc1,
    flat, part, scattered, near, far,
    in_sem, out_sem, halo_send, halo_recv, rs_send, rs_recv, y_send, y_recv, x_send, x_recv, ag_send, ag_recv,
):
    tm = lax.axis_index("tm")
    sp = lax.axis_index("space")
    up, down = lax.rem(sp + SPACE - 1, SPACE), lax.rem(sp + 1, SPACE)
    x, y = sp // RING, lax.rem(sp, RING)

    def y_peer(j):
        return x * RING + lax.rem(y + j, RING)

    def x_peer(j):
        return lax.rem(x + j, RING) * RING + y

    sources = ((cot_hbm, cot_in), (pre_hbm, pre_in), (feat_hbm, feat_in))

    def fetch(a, s):
        src, dst = sources[a]
        rows = pl.ds(al(s * STRIP, STRIP), STRIP)
        return pltpu.make_async_copy(src.at[:, rows, :], dst.at[:, rows, :], in_sem.at[a, s])

    for s in (0, 1, STRIPS - 1) + tuple(range(2, STRIPS - 1)):
        fetch(0, s).start()
        fetch(1, s).start()
    for s in range(STRIPS):
        fetch(2, s).start()

    barrier = pltpu.get_barrier_semaphore()
    for j in range(1, TM):
        pl.semaphore_signal(barrier, inc=1, device_id=(lax.rem(tm + j, TM), sp), device_id_type=MESH)
    for j in range(1, RING):
        pl.semaphore_signal(barrier, inc=1, device_id=(tm, y_peer(j)), device_id_type=MESH)
        pl.semaphore_signal(barrier, inc=1, device_id=(tm, x_peer(j)), device_id_type=MESH)
    for to in (up, down):
        pl.semaphore_signal(barrier, inc=1, device_id=(tm, to), device_id_type=MESH)

    build_mask(mask_ref, cells)
    build_weight(w2_ref, weight2)
    acc2[...] = jnp.zeros_like(acc2)
    acc1[...] = jnp.zeros_like(acc1)

    def strip_of(ref, s):
        mask = cells[pl.ds(s // 2, 1), :].astype(BF)
        return ref[:, pl.ds(al(s * STRIP, STRIP), STRIP), :], mask[None]

    def put(ref, first_row, s, x):
        x = jnp.transpose(x, (1, 0, 2)).reshape(STRIP * C, WIDTH)
        ref[pl.ds(al((s * STRIP + first_row) * C), STRIP * C), :] = x

    def load_cot_pre(s):
        v, mask = strip_of(cot_in, s)
        put(g, 2, s, v * mask)
        v, mask = strip_of(pre_in, s)
        put(kept, 1, s, jnp.maximum(v, jnp.zeros((), BF)) * mask)

    def load_feat(s):
        v, mask = strip_of(feat_in, s)
        put(inp, 0, s, v * mask)

    def halo(i, ref, src_row, dst_row, count, to):
        return pltpu.make_async_remote_copy(
            src_ref=ref.at[pl.ds(src_row * C, count * C), :],
            dst_ref=ref.at[pl.ds(dst_row * C, count * C), :],
            send_sem=halo_send.at[i],
            recv_sem=halo_recv.at[i],
            device_id=(tm, to),
            device_id_type=MESH,
        )

    halos = (
        halo(0, g, 2, ROWS + 2, 2, up),
        halo(1, g, ROWS, 0, 2, down),
        halo(2, kept, 1, ROWS + 1, 1, up),
        halo(3, kept, ROWS, 0, 1, down),
    )
    def second_conv(p):
        base = p * PAIR
        out = conv_pair(weight2[...], g, base).astype(BF)
        positive = kept[pl.ds(al(base), PAIR), :] > 0
        pgrad[pl.ds(al(base), PAIR), :] = jnp.where(positive, out, jnp.zeros((), BF))

    def second_grad(p):
        base = p * PAIR + C
        acc2[...] += grad_pair(kept, base, g, base)

    def pass1(s):
        for q in range(1, HALF + 1):
            second_conv(s * HALF + q)
            second_grad(s * HALF + q)

    def get_cot_pre(s):
        fetch(0, s).wait()
        fetch(1, s).wait()
        load_cot_pre(s)

    get_cot_pre(0)
    get_cot_pre(1)
    pass1(0)
    get_cot_pre(STRIPS - 1)
    pl.semaphore_wait(barrier, TM - 1 + 2 * (RING - 1) + 2)
    for h in halos:
        h.start()

    def body1(s, carry):
        get_cot_pre(s + 1)
        pass1(s)
        return carry

    lax.fori_loop(1, STRIPS - 2, body1, 0, unroll=True)
    pass1(STRIPS - 2)
    build_weight(w1_ref, weight1)
    for h in halos:
        h.wait()

    @pl.when(sp == 0)
    def _():
        g[pl.ds(0, 2 * C), :] = jnp.zeros((2 * C, WIDTH), BF)
        kept[pl.ds(0, C), :] = jnp.zeros((C, WIDTH), BF)

    @pl.when(sp == SPACE - 1)
    def _():
        g[pl.ds((ROWS + 2) * C, 2 * C), :] = jnp.zeros((2 * C, WIDTH), BF)
        kept[pl.ds((ROWS + 1) * C, C), :] = jnp.zeros((C, WIDTH), BF)

    for q in range(PAIRS - 7, PAIRS):
        second_conv(q)
        second_grad(q)
    for q in (0, PAIRS):
        second_conv(q)
    second_grad(0)

    def remote(src, dst, send, recv, to):
        return pltpu.make_async_remote_copy(
            src_ref=src, dst_ref=dst, send_sem=send, recv_sem=recv, device_id=to, device_id_type=MESH
        )

    def pack(n, acc):
        tail = []
        for s in range(3):
            top = acc[pl.ds(s * PAIR, C), :][:, : 3 * C]
            both = top + acc[pl.ds(s * PAIR + C, C), :][:, C:]
            flat[pl.ds(n * GRAD_ROWS + s * C, C), :] = both[:, :LANES]
            tail.append(both[:, LANES:])
        tail = jnp.concatenate(tail, axis=0)
        tail = jnp.concatenate([tail[: 3 * C // 2], tail[3 * C // 2 :]], axis=1)
        flat[pl.ds(n * GRAD_ROWS + 3 * C, 3 * C // 2), :] = tail

    scatter = []
    for j in range(1, TM):
        to = lax.rem(tm + j, TM)
        scatter.append(remote(part.at[to], scattered.at[j - 1], rs_send.at[j - 1], rs_recv.at[j - 1], (to, sp)))

    def cross_y(j, slot):
        slot = y if slot is None else lax.rem(y + j, RING)
        return remote(near.at[y], near.at[slot], y_send.at[j], y_recv.at[slot], (tm, y_peer(j)))

    def cross_x(j, slot):
        slot = x if slot is None else lax.rem(x + j, RING)
        return remote(far.at[x], far.at[slot], x_send.at[j], x_recv.at[slot], (tm, x_peer(j)))

    def spread(j, slot):
        to = lax.rem(tm + j, TM)
        slot = tm if slot is None else to
        return remote(total_ref.at[tm], total_ref.at[slot], ag_send.at[j], ag_recv.at[slot], (to, sp))

    def step1():
        for t in range(TM):
            own = jnp.concatenate([flat[pl.ds(t * USED, USED), :], jnp.zeros((CHUNK - USED, LANES), F32)], axis=0)
            part[t] = own.astype(BF)
        for c in scatter:
            c.start()

    def step2():
        for c in scatter:
            c.wait()
        mine = part[tm].astype(F32)
        for j in range(TM - 1):
            mine = mine + scattered[j].astype(F32)
        near[y] = mine.astype(BF)
        for j in range(1, RING):
            cross_y(j, None).start()

    def finish(cross, ref):
        for j in range(1, RING):
            cross(j, None).wait_send()
            cross(j, j).wait_recv()
        whole = ref[0].astype(F32)
        for j in range(1, RING):
            whole = whole + ref[j].astype(F32)
        return whole.astype(BF)

    def step3():
        far[x] = finish(cross_y, near)
        for j in range(1, RING):
            cross_x(j, None).start()

    def step4():
        total_ref[tm] = finish(cross_x, far)
        for j in range(1, TM):
            spread(j, None).start()

    def step5():
        for j in range(1, TM):
            spread(j, None).wait_send()
            spread(j, j).wait_recv()

    def pass2(s):
        for q in range(HALF):
            base = (s * HALF + q) * PAIR
            acc1[...] += grad_pair(inp, base, pgrad, base)

    def get_feat(s):
        fetch(2, s).wait()
        load_feat(s)

    def body2(s, carry):
        get_feat(s + 1)
        pass2(s)
        return carry

    get_feat(0)
    lax.fori_loop(0, STRIPS - 1, body2, 0, unroll=True)
    pass2(STRIPS - 1)
    pack(0, acc1)
    pack(1, acc2)
    step1()

    def store(s):
        r = pl.ds(al(s * STRIP, STRIP), STRIP)
        return pltpu.make_async_copy(cot_in.at[:, r, :], out_hbm.at[:, r, :], out_sem.at[s])

    def body3(s, carry):
        mask = cells[pl.ds(s // 2, 1), :]
        for q in range(HALF):
            base = (s * HALF + q) * PAIR
            kept[pl.ds(al(base), PAIR), :] = (conv_pair(weight1[...], pgrad, base) * mask).astype(BF)
        v = kept[pl.ds(al(s * STRIP * C), STRIP * C), :].reshape(STRIP, C, WIDTH)
        cot_in[:, pl.ds(al(s * STRIP, STRIP), STRIP), :] = jnp.transpose(v, (1, 0, 2))
        store(s).start()
        return carry

    lax.fori_loop(0, 3, body3, 0, unroll=True)
    step2()
    lax.fori_loop(3, 5, body3, 0, unroll=True)
    step3()
    body3(STRIPS - 1, 0)
    step4()
    for s in range(STRIPS):
        store(s).wait()
    step5()


def last_kernel(turned_ref, total_ref, out_hbm, first_ref, second_ref, sem):
    copies = []
    for s in range(PARTS):
        r = pl.ds(s * (C // PARTS), C // PARTS)
        copies.append(pltpu.make_async_copy(turned_ref.at[r], out_hbm.at[r], sem.at[s]))
        copies[-1].start()

    scale = 1.0 / math.sqrt(TM * ROWS * SPACE * WIDTH)
    flat = jnp.concatenate([total_ref[t].astype(F32)[:USED] for t in range(TM)], axis=0)
    for n, ref in enumerate((first_ref, second_ref)):
        rows = flat[n * GRAD_ROWS : (n + 1) * GRAD_ROWS]
        grid = rows[: 3 * C].T * scale
        for q in range(2):
            for s in range(3):
                ref[(2 - q) * 3 + s] = grid[q * C : (q + 1) * C, s * C : (s + 1) * C]
        grid = rows[3 * C :].T * scale
        h = C // 2
        ref[0] = grid[:C, :C]
        ref[1] = jnp.concatenate([grid[:C, C : C + h], grid[C:, :h]], axis=1)
        ref[2] = grid[C:, h : h + C]
    for c in copies:
        c.wait()


def block(features, pre_act, cotangent, first_weight, second_weight, tile_mask, tile_list):
    vmem = pl.BlockSpec(memory_space=pltpu.VMEM)
    hbm = pl.BlockSpec(memory_space=pl.ANY)
    shape = (C, ROWS, WIDTH)
    mask = tile_mask[0].T
    chunk = (CHUNK, LANES)
    dma = pltpu.SemaphoreType.DMA
    turned, total = pl.pallas_call(
        main_kernel,
        out_shape=(
            pltpu.VMEM(shape, BF),
            jax.ShapeDtypeStruct((TM,) + chunk, BF),
        ),
        in_specs=[hbm, hbm, hbm, vmem, vmem, vmem],
        out_specs=(hbm, vmem),
        scratch_shapes=[
            pltpu.VMEM(shape, BF),
            pltpu.VMEM(shape, BF),
            pltpu.VMEM(shape, BF),
            pltpu.VMEM(((ROWS + 4) * C, WIDTH), BF),
            pltpu.VMEM(((ROWS + 2) * C, WIDTH), BF),
            pltpu.VMEM((ROWS * C, WIDTH), BF),
            pltpu.VMEM(((ROWS + 2) * C, WIDTH), BF),
            pltpu.VMEM((3 * PAIR, 2 * PAIR), BF),
            pltpu.VMEM((3 * PAIR, 2 * PAIR), BF),
            pltpu.VMEM((8, WIDTH), F32),
            pltpu.VMEM((3 * PAIR, 2 * PAIR), F32),
            pltpu.VMEM((3 * PAIR, 2 * PAIR), F32),
            pltpu.VMEM((2 * GRAD_ROWS, LANES), F32),
            pltpu.VMEM((TM,) + chunk, BF),
            pltpu.VMEM((TM - 1,) + chunk, BF),
            pltpu.VMEM((RING,) + chunk, BF),
            pltpu.VMEM((RING,) + chunk, BF),
            dma((3, STRIPS)),
            dma((STRIPS,)),
            dma((4,)),
            dma((4,)),
            dma((TM - 1,)),
            dma((TM - 1,)),
            dma((RING,)),
            dma((RING,)),
            dma((RING,)),
            dma((RING,)),
            dma((TM,)),
            dma((TM,)),
        ],
        compiler_params=pltpu.CompilerParams(
            collective_id=0, has_side_effects=True, vmem_limit_bytes=52 * 2**20
        ),
        name="grads",
    )(cotangent[0], pre_act[0], features[0], second_weight, first_weight, mask)
    grad, first, second = pl.pallas_call(
        last_kernel,
        out_shape=(
            jax.ShapeDtypeStruct(shape, BF),
            jax.ShapeDtypeStruct((9, C, C), F32),
            jax.ShapeDtypeStruct((9, C, C), F32),
        ),
        in_specs=[hbm, vmem],
        out_specs=(hbm, vmem, vmem),
        scratch_shapes=[dma((PARTS,))],
        compiler_params=pltpu.CompilerParams(vmem_limit_bytes=8 * 2**20),
        name="input_grad",
    )(turned, total)
    return grad[None], first, second


def solution(mesh):
    return jax.shard_map(
        block,
        mesh=mesh,
        in_specs=(
            P("tm", None, "space", None),
            P("tm", None, "space", None),
            P("tm", None, "space", None),
            P(),
            P(),
            P("tm", None, None),
            P("tm", "space"),
        ),
        out_specs=(P("tm", None, "space", None), P(), P()),
        check_vma=False,
    )
```

```python
import math

import jax
import jax.numpy as jnp
from jax import lax
from jax.experimental import pallas as pl
from jax.experimental.pallas import tpu as pltpu
from jax.sharding import PartitionSpec as P

F32 = jnp.float32
BF = jnp.bfloat16
C = 64
TS = 32
ROWS = 96
WIDTH = 512
STRIP = 16
STRIPS = ROWS // STRIP
PAIR = 2 * C
PAIRS = ROWS // 2
TM = 8
SPACE = 16
HALF = STRIP // 2
LANES = 128
GRAD_ROWS = 9 * C // 2
USED = 2 * GRAD_ROWS // TM
CHUNK = 80
RING = 4
PARTS = 8
NT = (((1,), (1,)), ((), ()))
MESH = pl.DeviceIdType.MESH
ORDER = (1, 0, -1)


def al(x, m=C):
    return x if isinstance(x, int) else pl.multiple_of(x, m)


def shift_right(x):
    lane = lax.broadcasted_iota(jnp.int32, (x.shape[0], 128), 1)
    out, carry = [], None
    for j in range(x.shape[1] // 128):
        r = pltpu.roll(x[:, j * 128 : (j + 1) * 128], 1, 1)
        out.append(jnp.where(lane == 0, jnp.zeros_like(r) if carry is None else carry, r))
        carry = r
    return jnp.concatenate(out, axis=1)


def shift_left(x):
    lane = lax.broadcasted_iota(jnp.int32, (x.shape[0], 128), 1)
    out, carry = [], None
    for j in reversed(range(x.shape[1] // 128)):
        r = pltpu.roll(x[:, j * 128 : (j + 1) * 128], 127, 1)
        out.append(jnp.where(lane == 127, jnp.zeros_like(r) if carry is None else carry, r))
        carry = r
    return jnp.concatenate(out[::-1], axis=1)


def build_weight(w_ref, out_ref):
    zero = jnp.zeros((C, C), F32)
    rows = []
    for q in range(4):
        cols = []
        for dc in ORDER:
            for t in range(2):
                dr = t + 1 - q
                cols.append(w_ref[(dr + 1) * 3 + dc + 1].astype(F32) if abs(dr) <= 1 else zero)
        rows.append(jnp.concatenate(cols, axis=1))
    out_ref[...] = jnp.concatenate(rows, axis=0).T.astype(BF)


def build_mask(mask_ref, out_ref):
    first = lax.axis_index("space") * (ROWS // TS)
    cols, count = mask_ref.shape
    pick = lax.broadcasted_iota(jnp.int32, (8, count), 0) + first
    pick = (pick == lax.broadcasted_iota(jnp.int32, (8, count), 1)).astype(F32).astype(BF)
    own = lax.dot_general(pick, mask_ref[...].astype(F32).astype(BF), NT, preferred_element_type=F32)
    spread = lax.broadcasted_iota(jnp.int32, (cols, WIDTH), 1) >> 5
    spread = (spread == lax.broadcasted_iota(jnp.int32, (cols, WIDTH), 0)).astype(F32).astype(BF)
    out_ref[...] = jnp.dot(own.astype(BF), spread, preferred_element_type=F32)


def conv_pair(weight, src_ref, base):
    part = jnp.dot(weight, src_ref[pl.ds(al(base), 2 * PAIR), :], preferred_element_type=F32)
    return shift_right(part[:PAIR]) + part[PAIR : 2 * PAIR] + shift_left(part[2 * PAIR :])


def grad_pair(own_ref, own_base, src_ref, base):
    own = own_ref[pl.ds(al(own_base), PAIR), :]
    own = jnp.concatenate([shift_right(own), own, shift_left(own)], axis=0)
    return lax.dot_general(own, src_ref[pl.ds(al(base), 2 * PAIR), :], NT, preferred_element_type=F32)


def main_kernel(
    cot_hbm, pre_hbm, feat_hbm, w2_ref, w1_ref, mask_ref, out_hbm, total_ref,
    cot_in, pre_in, feat_in, g, kept, inp, pgrad, weight2, weight1, cells, acc2, acc1,
    flat, part, scattered, near, far,
    in_sem, out_sem, halo_send, halo_recv, rs_send, rs_recv, y_send, y_recv, x_send, x_recv, ag_send, ag_recv,
):
    tm = lax.axis_index("tm")
    sp = lax.axis_index("space")
    up, down = lax.rem(sp + SPACE - 1, SPACE), lax.rem(sp + 1, SPACE)
    x, y = sp // RING, lax.rem(sp, RING)

    def y_peer(j):
        return x * RING + lax.rem(y + j, RING)

    def x_peer(j):
        return lax.rem(x + j, RING) * RING + y

    sources = ((cot_hbm, cot_in), (pre_hbm, pre_in), (feat_hbm, feat_in))

    def fetch(a, s):
        src, dst = sources[a]
        rows = pl.ds(al(s * STRIP, STRIP), STRIP)
        return pltpu.make_async_copy(src.at[:, rows, :], dst.at[:, rows, :], in_sem.at[a, s])

    for s in (0, 1, STRIPS - 1) + tuple(range(2, STRIPS - 1)):
        fetch(0, s).start()
        fetch(1, s).start()
        if s == 1:
            fetch(2, 0).start()
    for s in range(1, STRIPS):
        fetch(2, s).start()

    barrier = pltpu.get_barrier_semaphore()
    for j in range(1, TM):
        pl.semaphore_signal(barrier, inc=1, device_id=(lax.rem(tm + j, TM), sp), device_id_type=MESH)
    for j in range(1, RING):
        pl.semaphore_signal(barrier, inc=1, device_id=(tm, y_peer(j)), device_id_type=MESH)
        pl.semaphore_signal(barrier, inc=1, device_id=(tm, x_peer(j)), device_id_type=MESH)
    for to in (up, down):
        pl.semaphore_signal(barrier, inc=1, device_id=(tm, to), device_id_type=MESH)

    build_mask(mask_ref, cells)
    build_weight(w2_ref, weight2)
    acc2[...] = jnp.zeros_like(acc2)
    acc1[...] = jnp.zeros_like(acc1)

    def strip_of(ref, s):
        mask = cells[pl.ds(s // 2, 1), :].astype(BF)
        return ref[:, pl.ds(al(s * STRIP, STRIP), STRIP), :], mask[None]

    def put(ref, first_row, s, x):
        x = jnp.transpose(x, (1, 0, 2)).reshape(STRIP * C, WIDTH)
        ref[pl.ds(al((s * STRIP + first_row) * C), STRIP * C), :] = x

    def load_cot_pre(s):
        v, mask = strip_of(cot_in, s)
        put(g, 2, s, v * mask)
        v, mask = strip_of(pre_in, s)
        put(kept, 1, s, jnp.maximum(v, jnp.zeros((), BF)) * mask)

    def load_feat(s):
        v, mask = strip_of(feat_in, s)
        put(inp, 0, s, v * mask)

    def halo(i, ref, src_row, dst_row, count, to):
        return pltpu.make_async_remote_copy(
            src_ref=ref.at[pl.ds(src_row * C, count * C), :],
            dst_ref=ref.at[pl.ds(dst_row * C, count * C), :],
            send_sem=halo_send.at[i],
            recv_sem=halo_recv.at[i],
            device_id=(tm, to),
            device_id_type=MESH,
        )

    halos = (
        halo(0, g, 2, ROWS + 2, 2, up),
        halo(1, g, ROWS, 0, 2, down),
        halo(2, kept, 1, ROWS + 1, 1, up),
        halo(3, kept, ROWS, 0, 1, down),
    )
    def second_conv(p):
        base = p * PAIR
        out = conv_pair(weight2[...], g, base).astype(BF)
        positive = kept[pl.ds(al(base), PAIR), :] > 0
        pgrad[pl.ds(al(base), PAIR), :] = jnp.where(positive, out, jnp.zeros((), BF))

    def second_grad(p):
        base = p * PAIR + C
        acc2[...] += grad_pair(kept, base, g, base)

    def first_grad(p):
        acc1[...] += grad_pair(inp, p * PAIR, pgrad, p * PAIR)

    def get_feat(s):
        fetch(2, s).wait()
        load_feat(s)

    def pass1(s):
        get_feat(s)
        for q in range(1, HALF + 1):
            second_conv(s * HALF + q)
            second_grad(s * HALF + q)
            if not isinstance(s, int) or s + q > 1:
                first_grad(s * HALF + q - 1)

    def get_cot_pre(s):
        fetch(0, s).wait()
        fetch(1, s).wait()
        load_cot_pre(s)

    get_cot_pre(0)
    get_cot_pre(1)
    pass1(0)
    get_cot_pre(STRIPS - 1)
    pl.semaphore_wait(barrier, TM - 1 + 2 * (RING - 1) + 2)
    for h in halos:
        h.start()

    def body1(s, carry):
        get_cot_pre(s + 1)
        pass1(s)
        return carry

    lax.fori_loop(1, STRIPS - 2, body1, 0, unroll=True)
    pass1(STRIPS - 2)
    build_weight(w1_ref, weight1)
    for h in halos:
        h.wait()

    @pl.when(sp == 0)
    def _():
        g[pl.ds(0, 2 * C), :] = jnp.zeros((2 * C, WIDTH), BF)
        kept[pl.ds(0, C), :] = jnp.zeros((C, WIDTH), BF)

    @pl.when(sp == SPACE - 1)
    def _():
        g[pl.ds((ROWS + 2) * C, 2 * C), :] = jnp.zeros((2 * C, WIDTH), BF)
        kept[pl.ds((ROWS + 1) * C, C), :] = jnp.zeros((C, WIDTH), BF)

    get_feat(STRIPS - 1)
    for q in range(PAIRS - 7, PAIRS):
        second_conv(q)
        second_grad(q)
        first_grad(q - 1)
    for q in (0, PAIRS):
        second_conv(q)
    second_grad(0)
    first_grad(0)
    first_grad(PAIRS - 1)

    def remote(src, dst, send, recv, to):
        return pltpu.make_async_remote_copy(
            src_ref=src, dst_ref=dst, send_sem=send, recv_sem=recv, device_id=to, device_id_type=MESH
        )

    def pack(n, acc):
        tail = []
        for s in range(3):
            top = acc[pl.ds(s * PAIR, C), :][:, : 3 * C]
            both = top + acc[pl.ds(s * PAIR + C, C), :][:, C:]
            flat[pl.ds(n * GRAD_ROWS + s * C, C), :] = both[:, :LANES]
            tail.append(both[:, LANES:])
        tail = jnp.concatenate(tail, axis=0)
        tail = jnp.concatenate([tail[: 3 * C // 2], tail[3 * C // 2 :]], axis=1)
        flat[pl.ds(n * GRAD_ROWS + 3 * C, 3 * C // 2), :] = tail

    scatter = []
    for j in range(1, TM):
        to = lax.rem(tm + j, TM)
        scatter.append(remote(part.at[to], scattered.at[j - 1], rs_send.at[j - 1], rs_recv.at[j - 1], (to, sp)))

    def cross_y(j, slot):
        slot = y if slot is None else lax.rem(y + j, RING)
        return remote(near.at[y], near.at[slot], y_send.at[j], y_recv.at[slot], (tm, y_peer(j)))

    def cross_x(j, slot):
        slot = x if slot is None else lax.rem(x + j, RING)
        return remote(far.at[x], far.at[slot], x_send.at[j], x_recv.at[slot], (tm, x_peer(j)))

    def spread(j, slot):
        to = lax.rem(tm + j, TM)
        slot = tm if slot is None else to
        return remote(total_ref.at[tm], total_ref.at[slot], ag_send.at[j], ag_recv.at[slot], (to, sp))

    def step1():
        for t in range(TM):
            own = jnp.concatenate([flat[pl.ds(t * USED, USED), :], jnp.zeros((CHUNK - USED, LANES), F32)], axis=0)
            part[t] = own.astype(BF)
        for c in scatter:
            c.start()

    def step2():
        for c in scatter:
            c.wait()
        mine = part[tm].astype(F32)
        for j in range(TM - 1):
            mine = mine + scattered[j].astype(F32)
        near[y] = mine.astype(BF)
        for j in range(1, RING):
            cross_y(j, None).start()

    def finish(cross, ref):
        for j in range(1, RING):
            cross(j, None).wait_send()
            cross(j, j).wait_recv()
        whole = ref[0].astype(F32)
        for j in range(1, RING):
            whole = whole + ref[j].astype(F32)
        return whole.astype(BF)

    def step3():
        far[x] = finish(cross_y, near)
        for j in range(1, RING):
            cross_x(j, None).start()

    def step4():
        total_ref[tm] = finish(cross_x, far)
        for j in range(1, TM):
            spread(j, None).start()

    def step5():
        for j in range(1, TM):
            spread(j, None).wait_send()
            spread(j, j).wait_recv()

    pack(0, acc1)
    pack(1, acc2)
    step1()

    def store(s):
        r = pl.ds(al(s * STRIP, STRIP), STRIP)
        return pltpu.make_async_copy(cot_in.at[:, r, :], out_hbm.at[:, r, :], out_sem.at[s])

    def body3(s, carry):
        mask = cells[pl.ds(s // 2, 1), :]
        for q in range(HALF):
            base = (s * HALF + q) * PAIR
            kept[pl.ds(al(base), PAIR), :] = (conv_pair(weight1[...], pgrad, base) * mask).astype(BF)
        v = kept[pl.ds(al(s * STRIP * C), STRIP * C), :].reshape(STRIP, C, WIDTH)
        cot_in[:, pl.ds(al(s * STRIP, STRIP), STRIP), :] = jnp.transpose(v, (1, 0, 2))
        store(s).start()
        return carry

    lax.fori_loop(0, 3, body3, 0, unroll=True)
    step2()
    lax.fori_loop(3, 5, body3, 0, unroll=True)
    step3()
    body3(STRIPS - 1, 0)
    step4()
    for s in range(STRIPS):
        store(s).wait()
    step5()


def last_kernel(turned_ref, total_ref, out_hbm, first_ref, second_ref, sem):
    copies = []
    for s in range(PARTS):
        r = pl.ds(s * (C // PARTS), C // PARTS)
        copies.append(pltpu.make_async_copy(turned_ref.at[r], out_hbm.at[r], sem.at[s]))
        copies[-1].start()

    scale = 1.0 / math.sqrt(TM * ROWS * SPACE * WIDTH)
    flat = jnp.concatenate([total_ref[t].astype(F32)[:USED] for t in range(TM)], axis=0)
    for n, ref in enumerate((first_ref, second_ref)):
        rows = flat[n * GRAD_ROWS : (n + 1) * GRAD_ROWS]
        grid = rows[: 3 * C].T * scale
        for q in range(2):
            for s in range(3):
                ref[(2 - q) * 3 + s] = grid[q * C : (q + 1) * C, s * C : (s + 1) * C]
        grid = rows[3 * C :].T * scale
        h = C // 2
        ref[0] = grid[:C, :C]
        ref[1] = jnp.concatenate([grid[:C, C : C + h], grid[C:, :h]], axis=1)
        ref[2] = grid[C:, h : h + C]
    for c in copies:
        c.wait()


def block(features, pre_act, cotangent, first_weight, second_weight, tile_mask, tile_list):
    vmem = pl.BlockSpec(memory_space=pltpu.VMEM)
    hbm = pl.BlockSpec(memory_space=pl.ANY)
    shape = (C, ROWS, WIDTH)
    mask = tile_mask[0].T
    chunk = (CHUNK, LANES)
    dma = pltpu.SemaphoreType.DMA
    turned, total = pl.pallas_call(
        main_kernel,
        out_shape=(
            pltpu.VMEM(shape, BF),
            jax.ShapeDtypeStruct((TM,) + chunk, BF),
        ),
        in_specs=[hbm, hbm, hbm, vmem, vmem, vmem],
        out_specs=(hbm, vmem),
        scratch_shapes=[
            pltpu.VMEM(shape, BF),
            pltpu.VMEM(shape, BF),
            pltpu.VMEM(shape, BF),
            pltpu.VMEM(((ROWS + 4) * C, WIDTH), BF),
            pltpu.VMEM(((ROWS + 2) * C, WIDTH), BF),
            pltpu.VMEM((ROWS * C, WIDTH), BF),
            pltpu.VMEM(((ROWS + 2) * C, WIDTH), BF),
            pltpu.VMEM((3 * PAIR, 2 * PAIR), BF),
            pltpu.VMEM((3 * PAIR, 2 * PAIR), BF),
            pltpu.VMEM((8, WIDTH), F32),
            pltpu.VMEM((3 * PAIR, 2 * PAIR), F32),
            pltpu.VMEM((3 * PAIR, 2 * PAIR), F32),
            pltpu.VMEM((2 * GRAD_ROWS, LANES), F32),
            pltpu.VMEM((TM,) + chunk, BF),
            pltpu.VMEM((TM - 1,) + chunk, BF),
            pltpu.VMEM((RING,) + chunk, BF),
            pltpu.VMEM((RING,) + chunk, BF),
            dma((3, STRIPS)),
            dma((STRIPS,)),
            dma((4,)),
            dma((4,)),
            dma((TM - 1,)),
            dma((TM - 1,)),
            dma((RING,)),
            dma((RING,)),
            dma((RING,)),
            dma((RING,)),
            dma((TM,)),
            dma((TM,)),
        ],
        compiler_params=pltpu.CompilerParams(
            collective_id=0, has_side_effects=True, vmem_limit_bytes=52 * 2**20
        ),
        name="grads",
    )(cotangent[0], pre_act[0], features[0], second_weight, first_weight, mask)
    grad, first, second = pl.pallas_call(
        last_kernel,
        out_shape=(
            jax.ShapeDtypeStruct(shape, BF),
            jax.ShapeDtypeStruct((9, C, C), F32),
            jax.ShapeDtypeStruct((9, C, C), F32),
        ),
        in_specs=[hbm, vmem],
        out_specs=(hbm, vmem, vmem),
        scratch_shapes=[dma((PARTS,))],
        compiler_params=pltpu.CompilerParams(vmem_limit_bytes=8 * 2**20),
        name="input_grad",
    )(turned, total)
    return grad[None], first, second


def solution(mesh):
    return jax.shard_map(
        block,
        mesh=mesh,
        in_specs=(
            P("tm", None, "space", None),
            P("tm", None, "space", None),
            P("tm", None, "space", None),
            P(),
            P(),
            P("tm", None, None),
            P("tm", "space"),
        ),
        out_specs=(P("tm", None, "space", None), P(), P()),
        check_vma=False,
    )
```
